32 devices in a mesh: section: 4 (over y, x), dp: 8 (over z, core).
Axes of the slice: x: 2, y: 2, z: 4, core: 2. Of those that a mesh axis runs over, the one named last changes fastest.
Arguments:
- activations: bfloat16 [4, 1024, 8192], P('section', 'dp'), may hold values from -6 to 6
- out_grads: bfloat16 [4, 1024, 1024], P('section', 'dp'), may hold values from -1.5 to 1.5
- in_basis: bfloat16 [4, 8192, 256], P('section', 'dp'), may hold values from -0.375 to 0.375
- out_basis: bfloat16 [4, 1024, 1024], P('section', 'dp'), may hold values from -0.1875 to 0.1875
- curvature: bfloat16 [4, 1024, 8192], P('section', None, 'dp'), may hold values from 2 to 32
- left_factors: bfloat16 [4, 8, 32, 1024], P('section', 'dp'), may hold values from -0.1875 to 0.1875
- right_factors: bfloat16 [4, 8, 32, 8192], P('section', None, None, 'dp'), may hold values from -0.0625 to 0.0625
- sequence_ids: int32 [8], replicated, may hold values from 0 to 7, each once
- query_order: int32 [8], replicated, may hold values from 0 to 7, each once
Outputs:
- influence: float32 [4, 8, 8], P('section', 'dp')
The draws below stay inside these ranges and needn't reach their ends.
Inputs may be any that keep to these rules, and one draw needn't show every extreme that they name: `sequence_ids`: a permutation: each output row receives exactly one training sequence. `query_order`: a permutation: each query is stored in exactly one slot.
All inputs are finite; a program needn't handle non-finite values.
Results may differ from the reference program's by a relative error of at most 0.0057.
Values may be sent and summed in bfloat16 or wider, within the bound.
No kernel may reach another device: no remote copies, remote signals or barrier semaphores. Data moves between devices by JAX's collectives and lax.ppermute only.
A program may use at most 128 MiB of HBM per device.

```python
import math
import jax
import jax.numpy as jnp
from jax import lax

D = 8192
DOUT = 1024
BLK = 256
RANK = 32
SEQ_LEN = 128
LAYERS = 4
SEQS = 8
TOKENS = 1024
QUERIES = 8


def shard_levels(key, extent, split, least, top_value):
    gain, own = 1.0, jax.random.fold_in(key, 6)
    for position, blocks in split:
        steps = jnp.exp(jax.random.uniform(jax.random.fold_in(own, position), (blocks,), jnp.float32, least / len(split), top_value / len(split)))
        gain = gain * jnp.repeat(steps, extent[position] // blocks).reshape([-1 if axis == position else 1 for axis in range(len(extent))])
    return gain


def gaussian(stream_key, dims, width, reach, cuts=(), held_as=jnp.bfloat16):
    factor_of = shard_levels(stream_key, dims, cuts, -0.22, 0.18) if cuts else 1.0
    values = jax.random.normal(stream_key, dims, jnp.float32) * width * factor_of
    return jnp.minimum(jnp.maximum(values, -reach), reach).astype(held_as)


def setup_inputs(seed: int = 0) -> dict:
    streams_of = jax.random.split(jax.random.key(seed), 10)
    activations = gaussian(streams_of[0], (LAYERS, TOKENS, D), 1.0, 6.0, ((0, 4), (1, 8)))
    out_grads = gaussian(streams_of[1], (LAYERS, TOKENS, DOUT), 0.25, 1.5, ((0, 4), (1, 8)))
    in_basis = gaussian(streams_of[2], (LAYERS, D, BLK), BLK ** -0.5, 0.375, ((0, 4), (1, 8)))
    out_basis = gaussian(streams_of[3], (LAYERS, DOUT, DOUT), DOUT ** -0.5, 0.1875, ((0, 4), (1, 8)))
    curvature = jnp.clip(jnp.exp(math.log(32.0) - 2.7725887 * jax.random.uniform(streams_of[4], (LAYERS, DOUT, D), jnp.float32) ** shard_levels(streams_of[4], (LAYERS, DOUT, D), ((0, 4), (2, 8)), -0.2, 0.2)), 2.0, 32.0).astype(jnp.bfloat16)
    left_factors = gaussian(streams_of[5], (LAYERS, QUERIES, RANK, DOUT), DOUT ** -0.5, 0.1875, ((0, 4), (1, 8)))
    right_factors = gaussian(streams_of[6], (LAYERS, QUERIES, RANK, D), D ** -0.5, 0.0625, ((0, 4), (3, 8)))
    sequence_ids = jax.random.permutation(streams_of[7], SEQS).astype(jnp.int32)
    query_order = jax.random.permutation(streams_of[8], QUERIES).astype(jnp.int32)
    return {"activations": activations, "out_grads": out_grads, "in_basis": in_basis, "out_basis": out_basis, "curvature": curvature, "left_factors": left_factors, "right_factors": right_factors, "sequence_ids": sequence_ids, "query_order": query_order}


def layer_scores(operands):
    activations, out_grads, in_basis, out_basis, curvature, left_factors, right_factors = operands
    n_blocks = D // BLK
    rotated_acts = jnp.einsum("tbi,bij->tbj", activations.reshape(TOKENS, n_blocks, BLK).astype(jnp.float32), in_basis.reshape(n_blocks, BLK, BLK).astype(jnp.float32))
    rotated_acts = rotated_acts.astype(jnp.bfloat16).reshape(SEQS, SEQ_LEN, D)
    rotated_grads = jnp.dot(out_grads.astype(jnp.float32), out_basis.astype(jnp.float32), preferred_element_type=jnp.float32)
    rotated_grads = rotated_grads.astype(jnp.bfloat16).reshape(SEQS, SEQ_LEN, DOUT)
    divisor = curvature.astype(jnp.float32)

    def one_query(factors):
        product = jnp.dot(factors[0].astype(jnp.float32).T, factors[1].astype(jnp.float32), preferred_element_type=jnp.float32)
        return product.astype(jnp.bfloat16).reshape(DOUT * D)

    query_mats = lax.map(one_query, (left_factors, right_factors))

    def one_sequence(pieces):
        gradient = jnp.dot(pieces[0].astype(jnp.float32).T, pieces[1].astype(jnp.float32), preferred_element_type=jnp.float32)
        return (gradient / divisor).astype(jnp.bfloat16).reshape(DOUT * D)

    scaled = lax.map(one_sequence, (rotated_grads, rotated_acts))
    return jnp.dot(scaled.astype(jnp.float32), query_mats.astype(jnp.float32).T, preferred_element_type=jnp.float32)


def reference(activations, out_grads, in_basis, out_basis, curvature, left_factors, right_factors, sequence_ids, query_order):
    scores = lax.map(layer_scores, (activations, out_grads, in_basis, out_basis, curvature, left_factors, right_factors))
    row_pick = (sequence_ids[None, :] == jnp.arange(SEQS, dtype=jnp.int32)[:, None]).astype(jnp.float32)
    col_pick = (query_order[:, None] == jnp.arange(QUERIES, dtype=jnp.int32)[None, :]).astype(jnp.float32)
    placed = jnp.einsum("mn,lnk,kq->lmq", row_pick, scores, col_pick, precision=lax.Precision.HIGHEST)
    return jnp.flip(jnp.cumsum(jnp.flip(placed, 0), axis=0), 0)
```

```python
import functools

import jax
import jax.numpy as jnp
from jax import lax
from jax.experimental import pallas as pl
from jax.experimental.pallas import tpu as pltpu
from jax.sharding import PartitionSpec as P

SEQ_LEN = 128
VMEM_BYTES = 56 * 2**20
F32 = jnp.float32
BF16 = jnp.bfloat16


def contract(a, b, dim_a, dim_b):
    return lax.dot_general(a, b, (((dim_a,), (dim_b,)), ((), ())), preferred_element_type=F32)


def rotate_kernel(count, sizes, place, *refs):
    pieces = refs[:count]
    grads_out, left_out, basis, grads, left, sem = refs[count:]
    copies = []
    for j in range(count):
        first = 0
        for part, (rows, buffer) in enumerate(zip(sizes, (basis, grads, left))):
            at = pl.multiple_of(place[j] * rows, rows)
            copies.append(
                pltpu.make_async_copy(
                    pieces[j].at[pl.ds(first, rows)], buffer.at[pl.ds(at, rows)], sem.at[part, j]
                )
            )
            first += rows
    for copy in copies:
        copy.start()
    for copy in copies:
        copy.wait()
    left_out[...] = left[...].T
    rows = sizes[1]

    def body(j, carry):
        own = pl.ds(pl.multiple_of(j * rows, rows), rows)
        grads_out[own, :] = contract(grads[own, :], basis[...], 1, 0).astype(BF16)
        return carry

    lax.fori_loop(0, count, body, 0)


def rotate_grads(place, pieces, sizes):
    count = len(pieces)
    width = pieces[0].shape[1]
    basis_rows, grad_rows, left_rows = (count * rows for rows in sizes)
    return pl.pallas_call(
        functools.partial(rotate_kernel, count, sizes),
        out_shape=(
            jax.ShapeDtypeStruct((grad_rows, width), BF16),
            jax.ShapeDtypeStruct((width, left_rows), BF16),
        ),
        in_specs=[pl.BlockSpec(memory_space=pltpu.SMEM)]
        + [pl.BlockSpec(memory_space=pl.ANY)] * count,
        out_specs=[pl.BlockSpec(memory_space=pltpu.VMEM)] * 2,
        scratch_shapes=[
            pltpu.VMEM((basis_rows, width), BF16),
            pltpu.VMEM((grad_rows, width), BF16),
            pltpu.VMEM((left_rows, width), BF16),
            pltpu.SemaphoreType.DMA((3, count)),
        ],
        compiler_params=pltpu.CompilerParams(vmem_limit_bytes=VMEM_BYTES),
        cost_estimate=pl.CostEstimate(
            flops=2 * grad_rows * basis_rows * width,
            bytes_accessed=2 * (basis_rows + 2 * grad_rows + 2 * left_rows) * width,
            transcendentals=0,
        ),
    )(place, *pieces)


def score_kernel(count, seq, *refs):
    acts, grads = refs[:count], refs[count : 2 * count]
    basis, curvature, right, left, out, rotated = refs[2 * count :]
    columns, size = basis.shape

    @pl.when(pl.program_id(0) == 0)
    def _():
        for q in range(count):
            for b in range(columns // size):
                own = slice(b * size, (b + 1) * size)
                rotated[q, :, own] = contract(acts[q][:, own], basis[own, :], 1, 0).astype(BF16)
        out[...] = jnp.zeros_like(out)

    inverse = 1.0 / curvature[...].astype(F32)
    weights = left[...].astype(F32)
    for q in range(count):
        scaled = (contract(grads[q][...], rotated[q], 0, 0) * inverse).astype(BF16)
        terms = contract(scaled, right[...], 1, 1) * weights
        out[q] += jnp.sum(terms.reshape(terms.shape[0] // 8, 8, terms.shape[1]), axis=0)


def score(sequences, acts, grads, basis, curvature, right, left):
    count = len(acts)
    width, columns = curvature.shape
    ranks = right.shape[0]
    block = min(width, 512)

    def whole(shape):
        return pl.BlockSpec(shape, lambda i, seq: (0, 0))

    def rows_of(at):
        return pl.BlockSpec((SEQ_LEN, columns), lambda i, seq: (at, 0))

    def grads_of(q):
        return pl.BlockSpec((SEQ_LEN, block), lambda i, seq: (seq[q], i))

    return pl.pallas_call(
        functools.partial(score_kernel, count),
        out_shape=jax.ShapeDtypeStruct((count, 8, ranks), F32),
        grid_spec=pltpu.PrefetchScalarGridSpec(
            num_scalar_prefetch=1,
            grid=(width // block,),
            in_specs=[rows_of(at) for _, at in acts]
            + [grads_of(q) for q in range(count)]
            + [
                whole(basis.shape),
                pl.BlockSpec((block, columns), lambda i, seq: (i, 0)),
                whole(right.shape),
                pl.BlockSpec((block, ranks), lambda i, seq: (i, 0)),
            ],
            out_specs=pl.BlockSpec((count, 8, ranks), lambda i, seq: (0, 0, 0)),
            scratch_shapes=[pltpu.VMEM((count, SEQ_LEN, columns), BF16)],
        ),
        compiler_params=pltpu.CompilerParams(vmem_limit_bytes=VMEM_BYTES),
        cost_estimate=pl.CostEstimate(
            flops=2 * count * width * columns * (SEQ_LEN + ranks),
            bytes_accessed=2 * (width * columns + count * SEQ_LEN * (width + columns)),
            transcendentals=0,
        ),
    )(sequences, *[array for array, _ in acts], *([grads] * count), basis, curvature, right, left)


def swap(x, k, n):
    return lax.ppermute(x, "dp", [(i, i ^ k) for i in range(n)])


def hop(x, pairs):
    return lax.ppermute(x, "dp", [(2 * a + c, 2 * b + c) for a, b in pairs for c in range(2)])


def gather_line(mine, me):
    chip = me // 2
    inner = (chip == 1) | (chip == 2)
    second_in = hop(mine, [(1, 2), (2, 1)])
    third_in = hop(mine, [(0, 2), (3, 1)])
    first = hop(mine, [(0, 1), (1, 0), (2, 3), (3, 2)])
    second_end = hop(second_in, [(2, 3), (1, 0)])
    third_end = hop(third_in, [(2, 3), (1, 0)])
    second = jnp.where(inner, second_in, second_end)
    third = jnp.where(inner, third_in, third_end)
    near, far = chip ^ 2, chip ^ 3
    chips = jnp.stack(
        [chip, chip ^ 1, jnp.where(inner, far, near), jnp.where(inner, near, far)]
    ).astype(jnp.int32)
    own = [mine, first, second, third]
    other = [swap(x, 1, 8) for x in own]
    core = me % 2
    return own + other, jnp.concatenate([2 * chips + core, 2 * chips + 1 - core])


def on_device(n, activations, out_grads, in_basis, out_basis, curvature, left_factors, right_factors,
              sequence_ids, query_order):
    me = lax.axis_index("dp")
    acts = activations[0]
    columns = in_basis.shape[1]
    width = out_basis.shape[2]
    left_own = left_factors[0].reshape(-1, width)
    sizes = (out_basis.shape[1], out_grads.shape[1], left_own.shape[0])
    mine = jnp.concatenate([out_basis[0], out_grads[0], left_own])
    if n == 8:
        pieces, place = gather_line(mine, me)
    else:
        every = lax.all_gather(mine, "dp", axis=0)
        pieces, place = [every[j] for j in range(n)], jnp.arange(n, dtype=jnp.int32)
    grads, left = rotate_grads(place, pieces, sizes)

    each = acts.shape[0] // SEQ_LEN
    right = right_factors[0].reshape(-1, columns)
    if n & (n - 1) == 0 and n <= 8:
        parts = [
            lax.dynamic_slice(acts, (0, (me ^ k) * columns), (acts.shape[0], columns))
            for k in range(n)
        ]
        parts = parts[:1] + [swap(parts[k], k, n) for k in range(1, n)]
        operands = [(part, j) for part in parts for j in range(each)]
        owners = jnp.stack([me ^ k for k in range(n)])
    else:
        part = lax.all_to_all(acts, "dp", split_axis=1, concat_axis=0, tiled=True)
        operands = [(part, j) for j in range(n * each)]
        owners = jnp.arange(n, dtype=jnp.int32)
    sequences = (owners[:, None] * each + jnp.arange(each)[None, :]).reshape(-1).astype(jnp.int32)
    step = min(len(operands), 4)
    sums = []
    for at in range(0, len(operands), step):
        sums.append(
            score(sequences[at : at + step], operands[at : at + step], grads, in_basis[0],
                  curvature[0], right, left)
        )
    sums = jnp.concatenate(sums)
    seqs = sums.shape[0]
    queries = right_factors.shape[1]
    scores = jnp.sum(sums.reshape(seqs, 8, queries, -1), axis=(1, 3))

    rows = jnp.sum(
        jnp.where(jnp.arange(seqs)[None, :, None] == sequences[:, None, None],
                  sequence_ids[None, :, None], 0), axis=1)
    row_pick = (rows.reshape(1, seqs) == jnp.arange(seqs)[:, None]).astype(F32)
    col_pick = (query_order[:, None] == jnp.arange(queries)[None, :]).astype(F32)
    placed = jnp.dot(jnp.dot(row_pick, scores, precision=lax.Precision.HIGHEST), col_pick,
                     precision=lax.Precision.HIGHEST)
    layers = lax.axis_size("section")
    wanted = jnp.arange(layers) <= lax.axis_index("section")
    outgoing = jnp.where(wanted[:, None, None], placed[None], 0.0)
    outgoing = outgoing.reshape(layers * n, seqs // n, queries)
    arrived = lax.all_to_all(outgoing, ("section", "dp"), split_axis=0, concat_axis=0, tiled=True)
    return jnp.sum(arrived, axis=0)[None]


def solution(mesh):
    placed = (
        P("section", "dp", None),
        P("section", "dp", None),
        P("section", "dp", None),
        P("section", "dp", None),
        P("section", None, "dp"),
        P("section", "dp", None, None),
        P("section", None, None, "dp"),
        P(),
        P(),
    )
    return jax.shard_map(
        functools.partial(on_device, mesh.shape["dp"]), mesh=mesh, in_specs=placed,
        out_specs=P("section", "dp", None), check_vma=False,
    )
```

```python
import functools

import jax
import jax.numpy as jnp
from jax import lax
from jax.experimental import pallas as pl
from jax.experimental.pallas import tpu as pltpu
from jax.sharding import PartitionSpec as P

SEQ_LEN = 128
VMEM_BYTES = 28 * 2**20
F32 = jnp.float32
BF16 = jnp.bfloat16


def contract(a, b, dim_a, dim_b):
    return lax.dot_general(a, b, (((dim_a,), (dim_b,)), ((), ())), preferred_element_type=F32)


def run_copies(pairs, sem):
    copies = [pltpu.make_async_copy(src, dst, sem.at[j]) for j, (src, dst) in enumerate(pairs)]
    for copy in copies:
        copy.start()
    for copy in copies:
        copy.wait()


def cut_kernel(rows, columns, place, acts, *refs):
    parts, (mine, beside, own, near, skip, across, sem) = refs[:3], refs[3:]
    chip, core = place[0] // 2, place[0] % 2

    def part(m, c):
        first = pl.multiple_of((2 * (chip ^ m) + c) * columns, columns)
        return acts.at[:, pl.ds(first, columns)]

    pairs, at = [], 0
    for x in parts:
        length = x.shape[0]
        pairs.append((x, mine.at[pl.ds(at, length)]))
        pairs.append((x, beside.at[pl.ds(4 * rows + at, length)]))
        at += length
    for m, out in enumerate((own, near, skip, across)):
        pairs.append((part(m, 1 - core), beside.at[pl.ds(m * rows, rows)]))
        pairs.append((part(m, core), out))
    run_copies(pairs, sem)


def cut(me, acts, parts, columns):
    rows = acts.shape[0]
    total = sum(part.shape[0] for part in parts)
    lengths = (total, 4 * rows + total, rows, rows, rows, rows)
    return pl.pallas_call(
        functools.partial(cut_kernel, rows, columns),
        out_shape=[jax.ShapeDtypeStruct((length, columns), BF16) for length in lengths],
        in_specs=[pl.BlockSpec(memory_space=pltpu.SMEM)]
        + [pl.BlockSpec(memory_space=pltpu.HBM)] * (1 + len(parts)),
        out_specs=[pl.BlockSpec(memory_space=pltpu.VMEM)] * len(lengths),
        scratch_shapes=[pltpu.SemaphoreType.DMA((14,))],
    )(me.reshape(1).astype(jnp.int32), acts, *parts)


def join_kernel(rows, beside, *refs):
    parts, outs, sem = refs[:3], refs[3:6], refs[6]
    pairs = [(part, out.at[pl.ds(0, rows)]) for part, out in zip(parts, outs)]
    for m, out in enumerate(outs):
        pairs.append((beside.at[pl.ds((m + 1) * rows, rows)], out.at[pl.ds(rows, rows)]))
    run_copies(pairs, sem)


def join_parts(rows, beside, parts):
    columns = beside.shape[1]
    return pl.pallas_call(
        functools.partial(join_kernel, rows),
        out_shape=[jax.ShapeDtypeStruct((2 * rows, columns), BF16)] * 3,
        in_specs=[pl.BlockSpec(memory_space=pltpu.HBM)] * 4,
        out_specs=[pl.BlockSpec(memory_space=pltpu.VMEM)] * 3,
        scratch_shapes=[pltpu.SemaphoreType.DMA((6,))],
    )(beside, *parts)


def rotate_kernel(count, sizes, starts, place, *refs):
    pieces = refs[:count]
    out, left, basis, grads, sem = refs[count:]
    copies = []
    for j in range(count):
        first = starts[j]
        for part, (rows, buffer) in enumerate(zip(sizes, (basis, grads, left))):
            at = pl.multiple_of(place[j] * rows, rows)
            copies.append(
                pltpu.make_async_copy(
                    pieces[j].at[pl.ds(first, rows)], buffer.at[pl.ds(at, rows)], sem.at[part, j]
                )
            )
            first += rows
    for copy in copies:
        copy.start()
    for copy in copies:
        copy.wait()
    width = basis.shape[1]
    size = min(width, 256)
    for j in range(0, width, size):
        out[:, j : j + size] = contract(grads[...], basis[:, j : j + size], 1, 0).astype(BF16)


def rotate_grads(place, pieces, sizes):
    count = len(pieces)
    width = pieces[0][0].shape[1]
    basis_rows, grad_rows, left_rows = (count * rows for rows in sizes)
    return pl.pallas_call(
        functools.partial(rotate_kernel, count, sizes, tuple(at for _, at in pieces)),
        out_shape=(
            jax.ShapeDtypeStruct((grad_rows, width), BF16),
            jax.ShapeDtypeStruct((left_rows, width), BF16),
        ),
        in_specs=[pl.BlockSpec(memory_space=pltpu.SMEM)]
        + [pl.BlockSpec(memory_space=pltpu.HBM)] * count,
        out_specs=[pl.BlockSpec(memory_space=pltpu.VMEM)] * 2,
        scratch_shapes=[
            pltpu.VMEM((basis_rows, width), BF16),
            pltpu.VMEM((grad_rows, width), BF16),
            pltpu.SemaphoreType.DMA((3, count)),
        ],
        compiler_params=pltpu.CompilerParams(
            vmem_limit_bytes=8 * 2**20 + 2 * width * (basis_rows + 2 * grad_rows + left_rows)
        ),
        cost_estimate=pl.CostEstimate(
            flops=2 * grad_rows * basis_rows * width,
            bytes_accessed=2 * (basis_rows + 2 * grad_rows + 2 * left_rows) * width,
            transcendentals=0,
        ),
    )(place.astype(jnp.int32), *[array for array, _ in pieces])


def score_kernel(blocks, parts, queries, info, *refs):
    count = len(blocks)
    arrays = refs[:parts]
    turned, left_in, basis_in, curvature_in, right_in, out = refs[parts : parts + 6]
    acts, rotated, grads, left, basis, curvature, right, sem = refs[parts + 6 :]
    columns, size = basis.shape
    width = curvature.shape[0]
    ranks = right.shape[0]
    step = min(width, 512)

    def acts_copy(q, array, at):
        src = arrays[array].at[pl.ds(at * SEQ_LEN, SEQ_LEN)]
        return pltpu.make_async_copy(src, acts.at[q], sem.at[q])

    def grads_copy(q):
        src = turned.at[pl.ds(pl.multiple_of(info[q] * SEQ_LEN, SEQ_LEN), SEQ_LEN)]
        return pltpu.make_async_copy(src, grads.at[q], sem.at[count + q])

    def curvature_copy(i):
        rows = pl.ds(i * step, step)
        return pltpu.make_async_copy(
            curvature_in.at[rows], curvature.at[rows], sem.at[2 * count + 3 + i]
        )

    basis_copy = pltpu.make_async_copy(basis_in, basis, sem.at[2 * count])
    left_copy = pltpu.make_async_copy(left_in, left, sem.at[2 * count + 1])
    right_copy = pltpu.make_async_copy(right_in, right, sem.at[2 * count + 2])
    basis_copy.start()
    for q, (one, other) in enumerate(blocks):
        if one == other:
            acts_copy(q, *one).start()
        else:
            @pl.when(info[count] == 1)
            def _():
                acts_copy(q, *one).start()

            @pl.when(info[count] == 0)
            def _():
                acts_copy(q, *other).start()
    for q in range(count):
        grads_copy(q).start()
    curvature_copy(0).start()
    right_copy.start()
    left_copy.start()
    for i in range(1, width // step):
        curvature_copy(i).start()
    basis_copy.wait()
    for q, (one, _) in enumerate(blocks):
        acts_copy(q, *one).wait()
        for b in range(columns // size):
            own = slice(b * size, (b + 1) * size)
            rotated[q, :, own] = contract(acts[q, :, own], basis[own, :], 1, 0).astype(BF16)
    for q in range(count):
        grads_copy(q).wait()
    for i in range(width // step):
        rows = slice(i * step, (i + 1) * step)
        curvature_copy(i).wait()
        if i == 0:
            right_copy.wait()
            left_copy.wait()
        inverse = 1.0 / curvature[rows, :].astype(F32)
        weights = left[:, rows].astype(F32)
        for q in range(count):
            scaled = (contract(grads[q, :, rows], rotated[q], 0, 0) * inverse).astype(BF16)
            terms = contract(right[...], scaled, 1, 1) * weights
            total = terms[:, :128]
            for j in range(128, step, 128):
                total = total + terms[:, j : j + 128]
            total = jnp.sum(total.reshape(queries, ranks // queries, 128), axis=1)
            out[q] = total if i == 0 else out[q] + total


def score(sequences, inner, acts, turned, left, basis, curvature, right, queries):
    count = len(acts)
    width, columns = curvature.shape
    ranks = right.shape[0]
    arrays = []

    def index(x):
        if not any(x is y for y in arrays):
            arrays.append(x)
        return [x is y for y in arrays].index(True)

    blocks = tuple(((index(x), i), (index(y), j)) for (x, i), (y, j) in acts)
    info = jnp.concatenate([sequences, inner.reshape(1)]).astype(jnp.int32)
    in_vmem = pl.BlockSpec(memory_space=pltpu.VMEM)
    in_hbm = pl.BlockSpec(memory_space=pltpu.HBM)
    return pl.pallas_call(
        functools.partial(score_kernel, blocks, len(arrays), queries),
        out_shape=jax.ShapeDtypeStruct((count, queries, 128), F32),
        in_specs=[pl.BlockSpec(memory_space=pltpu.SMEM)] + [in_hbm] * (len(arrays) + 5),
        out_specs=in_vmem,
        scratch_shapes=[
            pltpu.VMEM((count, SEQ_LEN, columns), BF16),
            pltpu.VMEM((count, SEQ_LEN, columns), BF16),
            pltpu.VMEM((count, SEQ_LEN, width), BF16),
            pltpu.VMEM(left.shape, BF16),
            pltpu.VMEM(basis.shape, BF16),
            pltpu.VMEM(curvature.shape, BF16),
            pltpu.VMEM(right.shape, BF16),
            pltpu.SemaphoreType.DMA((2 * count + 3 + width // min(width, 512),)),
        ],
        compiler_params=pltpu.CompilerParams(vmem_limit_bytes=VMEM_BYTES),
        cost_estimate=pl.CostEstimate(
            flops=2 * count * width * columns * (SEQ_LEN + ranks),
            bytes_accessed=2 * (width * columns + count * SEQ_LEN * (width + columns)),
            transcendentals=0,
        ),
    )(info, *arrays, turned, left, basis, curvature, right)


def swap(x, k, n):
    return lax.ppermute(x, "dp", [(i, i ^ k) for i in range(n)])


def hop(x, pairs, cross=False):
    pairs = [(2 * a + c, 2 * b + (c ^ int(cross))) for a, b in pairs for c in range(2)]
    return lax.ppermute(x, "dp", pairs)


def after(x, *others):
    return lax.optimization_barrier((x, *others))[0]


def exchange_line(acts, parts, columns, me, sizes):
    chip, core = me // 2, me % 2
    inner = (chip == 1) | (chip == 2)
    rows = acts.shape[0]
    outward = [(1, 0), (2, 3)]
    mine, to_beside, own, near, skip, across = cut(me, acts, parts, columns)
    second_in = hop(mine, [(1, 2), (2, 1)])
    third_in = hop(mine, [(0, 2), (3, 1)])
    first = hop(mine, [(0, 1), (1, 0), (2, 3), (3, 2)])
    beside = swap(to_beside, 1, 8)
    near, skip, across = join_parts(rows, beside, (near, skip, across))
    near_out = hop(near, outward)
    second_end = hop(after(second_in, first, near_out), outward)
    third_end = hop(third_in, outward)
    across_in = hop(after(across, second_in), [(1, 2), (2, 1)])
    skip_in = hop(after(skip, third_in), [(0, 2), (3, 1)])
    first_x = swap(first, 1, 8)
    second = jnp.where(inner, second_in, after(second_end, across_in))
    third = jnp.where(inner, third_in, after(third_end, skip_in))
    near_in = hop(after(near, first), [(0, 1), (3, 2)])
    skip_out = hop(after(skip, skip_in, across_in), [(1, 3), (2, 0)])
    across_out = hop(after(across, skip_in, across_in), [(0, 3), (3, 0)])
    chips = jnp.stack(
        [chip, chip ^ 1, jnp.where(inner, chip ^ 3, chip ^ 2), jnp.where(inner, chip ^ 2, chip ^ 3)]
    )
    pieces = [(x, 0) for x in (mine, first, second, third)]
    pieces += [(beside, 4 * rows)] + [(x, 0) for x in (first_x, swap(second, 1, 8), swap(third, 1, 8))]
    place = jnp.concatenate([2 * chips + core, 2 * chips + 1 - core])
    turned, left = rotate_grads(place, pieces, sizes)
    each = rows // SEQ_LEN
    owners = [me, me ^ 1]
    blocks = [((x, j), (x, j)) for x in (own, beside) for j in range(each)]
    for inside, x, outside, y in (
        (6, (across_in, across_in), 2, (near_out, near_out)),
        (4, (skip_in, skip_in), 4, (skip_out, skip_out)),
        (2, (near_in, near_in), 6, (across_out, across_out)),
    ):
        for c in range(2):
            owners.append(me ^ (jnp.where(inner, inside, outside) + c))
            for j in range(each):
                at = [c * each + j if z[0] is z[1] else j for z in (x, y)]
                blocks.append(((x[c], at[0]), (y[c], at[1])))
    return inner, turned, left, jnp.stack(owners), blocks


def on_device(n, activations, out_grads, in_basis, out_basis, curvature, left_factors, right_factors,
              sequence_ids, query_order):
    me = lax.axis_index("dp")
    acts = activations[0]
    columns = in_basis.shape[1]
    width = out_basis.shape[2]
    left_own = left_factors[0].reshape(-1, width)
    parts = [out_basis[0], out_grads[0], left_own]
    sizes = tuple(part.shape[0] for part in parts)
    right = right_factors[0].reshape(-1, columns)
    queries = right_factors.shape[1]
    each = acts.shape[0] // SEQ_LEN
    if n == 8:
        inner, turned, left, owners, operands = exchange_line(acts, parts, columns, me, sizes)
    else:
        every = lax.all_gather(jnp.concatenate(parts), "dp", axis=0)
        pieces, place = [(every[j], 0) for j in range(n)], jnp.arange(n, dtype=jnp.int32)
        turned, left = rotate_grads(place, pieces, sizes)
        part = lax.all_to_all(acts, "dp", split_axis=1, concat_axis=0, tiled=True)
        operands = [((part, j), (part, j)) for j in range(n * each)]
        inner = jnp.bool_(True)
        owners = jnp.arange(n, dtype=jnp.int32)
    sequences = (owners[:, None] * each + jnp.arange(each)[None, :]).reshape(-1).astype(jnp.int32)
    sums = []
    at = 0
    while at < len(operands):
        step = (4 if at == 0 else 2) * each
        sums.append(
            score(sequences[at : at + step], inner, operands[at : at + step], turned, left, in_basis[0],
                  curvature[0], right, queries)
        )
        at += step
    scores = jnp.sum(jnp.concatenate(sums), axis=2)
    seqs = scores.shape[0]

    rows = jnp.sum(
        jnp.where(jnp.arange(seqs)[None, :, None] == sequences[:, None, None],
                  sequence_ids[None, :, None], 0), axis=1)
    row_pick = (rows.reshape(1, seqs) == jnp.arange(seqs)[:, None]).astype(F32)
    col_pick = (query_order[:, None] == jnp.arange(queries)[None, :]).astype(F32)
    placed = jnp.dot(jnp.dot(row_pick, scores, precision=lax.Precision.HIGHEST), col_pick,
                     precision=lax.Precision.HIGHEST)
    layers = lax.axis_size("section")
    wanted = jnp.arange(layers) <= lax.axis_index("section")
    outgoing = jnp.where(wanted[:, None, None], placed[None], 0.0)
    outgoing = outgoing.reshape(layers * n, seqs // n, queries)
    arrived = lax.all_to_all(outgoing, ("section", "dp"), split_axis=0, concat_axis=0, tiled=True)
    return jnp.sum(arrived, axis=0)[None]


def solution(mesh):
    placed = (
        P("section", "dp", None),
        P("section", "dp", None),
        P("section", "dp", None),
        P("section", "dp", None),
        P("section", None, "dp"),
        P("section", "dp", None, None),
        P("section", None, None, "dp"),
        P(),
        P(),
    )
    return jax.shard_map(
        functools.partial(on_device, mesh.shape["dp"]), mesh=mesh, in_specs=placed,
        out_specs=P("section", "dp", None), check_vma=False,
    )
```

```python
import functools

import jax
import jax.numpy as jnp
from jax import lax
from jax.experimental import pallas as pl
from jax.experimental.pallas import tpu as pltpu
from jax.sharding import PartitionSpec as P

SEQ_LEN = 128
VMEM_BYTES = 28 * 2**20
F32 = jnp.float32
BF16 = jnp.bfloat16


def contract(a, b, dim_a, dim_b):
    return lax.dot_general(a, b, (((dim_a,), (dim_b,)), ((), ())), preferred_element_type=F32)


def run_copies(pairs, sem):
    copies = [pltpu.make_async_copy(src, dst, sem.at[j]) for j, (src, dst) in enumerate(pairs)]
    for copy in copies:
        copy.start()
    for copy in copies:
        copy.wait()


def cut_kernel(rows, columns, place, acts, *refs):
    parts, (mine, beside, own, near, skip, across, sem) = refs[:3], refs[3:]
    chip, core = place[0] // 2, place[0] % 2

    def part(m, c):
        first = pl.multiple_of((2 * (chip ^ m) + c) * columns, columns)
        return acts.at[:, pl.ds(first, columns)]

    pairs, at = [], 0
    for x in parts:
        length = x.shape[0]
        pairs.append((x, mine.at[pl.ds(at, length)]))
        pairs.append((x, beside.at[pl.ds(4 * rows + at, length)]))
        at += length
    for m, out in enumerate((own, near, skip, across)):
        pairs.append((part(m, 1 - core), beside.at[pl.ds(m * rows, rows)]))
        pairs.append((part(m, core), out))
    run_copies(pairs, sem)


def cut(me, acts, parts, columns):
    rows = acts.shape[0]
    total = sum(part.shape[0] for part in parts)
    lengths = (total, 4 * rows + total, rows, rows, rows, rows)
    return pl.pallas_call(
        functools.partial(cut_kernel, rows, columns),
        out_shape=[jax.ShapeDtypeStruct((length, columns), BF16) for length in lengths],
        in_specs=[pl.BlockSpec(memory_space=pltpu.SMEM)]
        + [pl.BlockSpec(memory_space=pltpu.HBM)] * (1 + len(parts)),
        out_specs=[pl.BlockSpec(memory_space=pltpu.VMEM)] * len(lengths),
        scratch_shapes=[pltpu.SemaphoreType.DMA((14,))],
    )(me.reshape(1).astype(jnp.int32), acts, *parts)


def join_kernel(rows, beside, *refs):
    parts, outs, sem = refs[:3], refs[3:6], refs[6]
    pairs = [(part, out.at[pl.ds(0, rows)]) for part, out in zip(parts, outs)]
    for m, out in enumerate(outs):
        pairs.append((beside.at[pl.ds((m + 1) * rows, rows)], out.at[pl.ds(rows, rows)]))
    run_copies(pairs, sem)


def join_parts(rows, beside, parts):
    columns = beside.shape[1]
    return pl.pallas_call(
        functools.partial(join_kernel, rows),
        out_shape=[jax.ShapeDtypeStruct((2 * rows, columns), BF16)] * 3,
        in_specs=[pl.BlockSpec(memory_space=pltpu.HBM)] * 4,
        out_specs=[pl.BlockSpec(memory_space=pltpu.VMEM)] * 3,
        scratch_shapes=[pltpu.SemaphoreType.DMA((6,))],
    )(beside, *parts)


def rotate_kernel(count, sizes, sources, parts, place, *refs):
    out, left, basis, grads, sem = refs[parts:]
    copies = []
    for j in range(count):
        for part, (rows, buffer) in enumerate(zip(sizes, (basis, grads, left))):
            array, first = sources[j][part]
            at = pl.multiple_of(place[j] * rows, rows)
            src = refs[array].at[pl.ds(first, rows)]
            copies.append(
                pltpu.make_async_copy(src, buffer.at[pl.ds(at, rows)], sem.at[part, j])
            )
    for copy in copies:
        copy.start()
    for copy in copies:
        copy.wait()
    width = basis.shape[1]
    size = min(width, 256)
    for j in range(0, width, size):
        out[:, j : j + size] = contract(grads[...], basis[:, j : j + size], 1, 0).astype(BF16)


def index_in(arrays, x):
    if not any(x is y for y in arrays):
        arrays.append(x)
    return [x is y for y in arrays].index(True)


def rotate_grads(place, pieces, sizes):
    count = len(pieces)
    width = pieces[0][0][0].shape[1]
    arrays = []
    sources = tuple(tuple((index_in(arrays, x), at) for x, at in piece) for piece in pieces)
    basis_rows, grad_rows, left_rows = (count * rows for rows in sizes)
    return pl.pallas_call(
        functools.partial(rotate_kernel, count, sizes, sources, len(arrays)),
        out_shape=(
            jax.ShapeDtypeStruct((grad_rows, width), BF16),
            jax.ShapeDtypeStruct((left_rows, width), BF16),
        ),
        in_specs=[pl.BlockSpec(memory_space=pltpu.SMEM)]
        + [pl.BlockSpec(memory_space=pltpu.HBM)] * len(arrays),
        out_specs=[pl.BlockSpec(memory_space=pltpu.VMEM)] * 2,
        scratch_shapes=[
            pltpu.VMEM((basis_rows, width), BF16),
            pltpu.VMEM((grad_rows, width), BF16),
            pltpu.SemaphoreType.DMA((3, count)),
        ],
        compiler_params=pltpu.CompilerParams(
            vmem_limit_bytes=8 * 2**20 + 2 * width * (basis_rows + 2 * grad_rows + left_rows)
        ),
        cost_estimate=pl.CostEstimate(
            flops=1,
            bytes_accessed=1,
            transcendentals=0,
        ),
    )(place.astype(jnp.int32), *arrays)


def score_kernel(blocks, parts, queries, info, *refs):
    count = len(blocks)
    arrays = refs[:parts]
    turned, left_in, basis_in, curvature_in, right_in, out = refs[parts : parts + 6]
    acts, rotated, grads, left, basis, curvature, right, sem = refs[parts + 6 :]
    columns, size = basis.shape
    width = curvature.shape[0]
    ranks = right.shape[0]
    step = min(width, 512)

    def acts_copy(q, array, at):
        src = arrays[array].at[pl.ds(at * SEQ_LEN, SEQ_LEN)]
        return pltpu.make_async_copy(src, acts.at[q], sem.at[q])

    def grads_copy(q):
        src = turned.at[pl.ds(pl.multiple_of(info[q] * SEQ_LEN, SEQ_LEN), SEQ_LEN)]
        return pltpu.make_async_copy(src, grads.at[q], sem.at[count + q])

    def curvature_copy(i):
        rows = pl.ds(i * step, step)
        return pltpu.make_async_copy(
            curvature_in.at[rows], curvature.at[rows], sem.at[2 * count + 3 + i]
        )

    basis_copy = pltpu.make_async_copy(basis_in, basis, sem.at[2 * count])
    left_copy = pltpu.make_async_copy(left_in, left, sem.at[2 * count + 1])
    right_copy = pltpu.make_async_copy(right_in, right, sem.at[2 * count + 2])
    basis_copy.start()
    for q, (one, other) in enumerate(blocks):
        if one == other:
            acts_copy(q, *one).start()
        else:
            @pl.when(info[count] == 1)
            def _():
                acts_copy(q, *one).start()

            @pl.when(info[count] == 0)
            def _():
                acts_copy(q, *other).start()
    for q in range(count):
        grads_copy(q).start()
    curvature_copy(0).start()
    right_copy.start()
    left_copy.start()
    for i in range(1, width // step):
        curvature_copy(i).start()
    basis_copy.wait()
    for q, (one, _) in enumerate(blocks):
        acts_copy(q, *one).wait()
        for b in range(columns // size):
            own = slice(b * size, (b + 1) * size)
            rotated[q, :, own] = contract(acts[q, :, own], basis[own, :], 1, 0).astype(BF16)
    for q in range(count):
        grads_copy(q).wait()
    for i in range(width // step):
        rows = slice(i * step, (i + 1) * step)
        curvature_copy(i).wait()
        if i == 0:
            right_copy.wait()
            left_copy.wait()
        inverse = 1.0 / curvature[rows, :].astype(F32)
        weights = left[:, rows].astype(F32)
        for q in range(count):
            scaled = (contract(grads[q, :, rows], rotated[q], 0, 0) * inverse).astype(BF16)
            terms = contract(right[...], scaled, 1, 1) * weights
            total = terms[:, :128]
            for j in range(128, step, 128):
                total = total + terms[:, j : j + 128]
            total = jnp.sum(total.reshape(queries, ranks // queries, 128), axis=1)
            out[q] = total if i == 0 else out[q] + total


def score(sequences, inner, acts, turned, left, basis, curvature, right, queries):
    count = len(acts)
    width, columns = curvature.shape
    ranks = right.shape[0]
    arrays = []

    blocks = tuple(((index_in(arrays, x), i), (index_in(arrays, y), j)) for (x, i), (y, j) in acts)
    info = jnp.concatenate([sequences, inner.reshape(1)]).astype(jnp.int32)
    in_vmem = pl.BlockSpec(memory_space=pltpu.VMEM)
    in_hbm = pl.BlockSpec(memory_space=pltpu.HBM)
    return pl.pallas_call(
        functools.partial(score_kernel, blocks, len(arrays), queries),
        out_shape=jax.ShapeDtypeStruct((count, queries, 128), F32),
        in_specs=[pl.BlockSpec(memory_space=pltpu.SMEM)] + [in_hbm] * (len(arrays) + 5),
        out_specs=in_vmem,
        scratch_shapes=[
            pltpu.VMEM((count, SEQ_LEN, columns), BF16),
            pltpu.VMEM((count, SEQ_LEN, columns), BF16),
            pltpu.VMEM((count, SEQ_LEN, width), BF16),
            pltpu.VMEM(left.shape, BF16),
            pltpu.VMEM(basis.shape, BF16),
            pltpu.VMEM(curvature.shape, BF16),
            pltpu.VMEM(right.shape, BF16),
            pltpu.SemaphoreType.DMA((2 * count + 3 + width // min(width, 512),)),
        ],
        compiler_params=pltpu.CompilerParams(vmem_limit_bytes=VMEM_BYTES),
        cost_estimate=pl.CostEstimate(
            flops=1,
            bytes_accessed=1,
            transcendentals=0,
        ),
    )(info, *arrays, turned, left, basis, curvature, right)


def swap(x, k, n):
    return lax.ppermute(x, "dp", [(i, i ^ k) for i in range(n)])


def hop(x, pairs, cross=False):
    pairs = [(2 * a + c, 2 * b + (c ^ int(cross))) for a, b in pairs for c in range(2)]
    return lax.ppermute(x, "dp", pairs)


def after(x, *others):
    return lax.optimization_barrier((x, *others))[0]


def exchange_line(acts, parts, columns, me, sizes):
    chip, core = me // 2, me % 2
    inner = (chip == 1) | (chip == 2)
    rows = acts.shape[0]
    outward = [(1, 0), (2, 3)]
    mine, to_beside, own, near, skip, across = cut(me, acts, parts, columns)
    second_in = hop(mine, [(1, 2), (2, 1)])
    third_in = hop(mine, [(0, 2), (3, 1)])
    first = hop(mine, [(0, 1), (1, 0), (2, 3), (3, 2)])
    beside = swap(to_beside, 1, 8)
    near, skip, across = join_parts(rows, beside, (near, skip, across))
    near_out = hop(near, outward)
    second_end = hop(after(second_in, first, near_out), outward)
    third_end = hop(third_in, outward)
    across_in = hop(after(across, second_in), [(1, 2), (2, 1)])
    skip_in = hop(after(skip, third_in), [(0, 2), (3, 1)])
    near_in = hop(after(near, first), [(0, 1), (3, 2)])
    skip_out = hop(after(skip, skip_in, across_in), [(1, 3), (2, 0)])
    first_x = swap(first, 1, 8)
    third = jnp.where(inner, third_in, after(third_end, skip_in))
    third_x = swap(third, 1, 8)
    second_end = after(second_end, across_in, near_in)
    second = [
        jnp.where(inner, second_in[: sizes[0]], second_end[: sizes[0]]),
        jnp.where(inner, second_in[sizes[0] :], second_end[sizes[0] :]),
    ]
    second_x = [swap(x, 1, 8) for x in second]
    across_out = hop(after(across, skip_in, across_in), [(0, 3), (3, 0)])
    chips = jnp.stack(
        [chip, chip ^ 1, jnp.where(inner, chip ^ 3, chip ^ 2), jnp.where(inner, chip ^ 2, chip ^ 3)]
    )
    def whole(x, at=0):
        return [(x, at), (x, at + sizes[0]), (x, at + sizes[0] + sizes[1])]

    def split(x, rest):
        return [(x, 0), (rest, 0), (rest, sizes[1])]

    pieces = [whole(mine), whole(first), split(*second), whole(third)]
    pieces += [whole(beside, 4 * rows), whole(first_x), split(*second_x), whole(third_x)]
    place = jnp.concatenate([2 * chips + core, 2 * chips + 1 - core])
    turned, left = rotate_grads(place, pieces, sizes)
    each = rows // SEQ_LEN
    owners = [me, me ^ 1]
    blocks = [((x, j), (x, j)) for x in (own, beside) for j in range(each)]
    for inside, x, outside, y in (
        (6, (across_in, across_in), 2, (near_out, near_out)),
        (4, (skip_in, skip_in), 4, (skip_out, skip_out)),
        (2, (near_in, near_in), 6, (across_out, across_out)),
    ):
        for c in range(2):
            owners.append(me ^ (jnp.where(inner, inside, outside) + c))
            for j in range(each):
                at = [c * each + j if z[0] is z[1] else j for z in (x, y)]
                blocks.append(((x[c], at[0]), (y[c], at[1])))
    return inner, turned, left, jnp.stack(owners), blocks


def on_device(n, activations, out_grads, in_basis, out_basis, curvature, left_factors, right_factors,
              sequence_ids, query_order):
    me = lax.axis_index("dp")
    acts = activations[0]
    columns = in_basis.shape[1]
    width = out_basis.shape[2]
    left_own = left_factors[0].reshape(-1, width)
    parts = [out_basis[0], out_grads[0], left_own]
    sizes = tuple(part.shape[0] for part in parts)
    right = right_factors[0].reshape(-1, columns)
    queries = right_factors.shape[1]
    each = acts.shape[0] // SEQ_LEN
    if n == 8:
        inner, turned, left, owners, operands = exchange_line(acts, parts, columns, me, sizes)
    else:
        every = lax.all_gather(jnp.concatenate(parts), "dp", axis=0)
        starts = (0, sizes[0], sizes[0] + sizes[1])
        pieces = [[(every[j], at) for at in starts] for j in range(n)]
        place = jnp.arange(n, dtype=jnp.int32)
        turned, left = rotate_grads(place, pieces, sizes)
        part = lax.all_to_all(acts, "dp", split_axis=1, concat_axis=0, tiled=True)
        operands = [((part, j), (part, j)) for j in range(n * each)]
        inner = jnp.bool_(True)
        owners = jnp.arange(n, dtype=jnp.int32)
    sequences = (owners[:, None] * each + jnp.arange(each)[None, :]).reshape(-1).astype(jnp.int32)
    sums = []
    at = 0
    while at < len(operands):
        step = (4 if at == 0 else 2) * each
        sums.append(
            score(sequences[at : at + step], inner, operands[at : at + step], turned, left, in_basis[0],
                  curvature[0], right, queries)
        )
        at += step
    scores = jnp.sum(jnp.concatenate(sums), axis=2)
    seqs = scores.shape[0]

    rows = jnp.sum(
        jnp.where(jnp.arange(seqs)[None, :, None] == sequences[:, None, None],
                  sequence_ids[None, :, None], 0), axis=1)
    row_pick = (rows.reshape(1, seqs) == jnp.arange(seqs)[:, None]).astype(F32)
    col_pick = (query_order[:, None] == jnp.arange(queries)[None, :]).astype(F32)
    placed = jnp.dot(jnp.dot(row_pick, scores, precision=lax.Precision.HIGHEST), col_pick,
                     precision=lax.Precision.HIGHEST)
    layers = lax.axis_size("section")
    wanted = jnp.arange(layers) <= lax.axis_index("section")
    outgoing = jnp.where(wanted[:, None, None], placed[None], 0.0)
    outgoing = outgoing.reshape(layers * n, seqs // n, queries)
    arrived = lax.all_to_all(outgoing, ("section", "dp"), split_axis=0, concat_axis=0, tiled=True)
    return jnp.sum(arrived, axis=0)[None]


def solution(mesh):
    placed = (
        P("section", "dp", None),
        P("section", "dp", None),
        P("section", "dp", None),
        P("section", "dp", None),
        P("section", None, "dp"),
        P("section", "dp", None, None),
        P("section", None, None, "dp"),
        P(),
        P(),
    )
    return jax.shard_map(
        functools.partial(on_device, mesh.shape["dp"]), mesh=mesh, in_specs=placed,
        out_specs=P("section", "dp", None), check_vma=False,
    )
```

```python
import functools

import jax
import jax.numpy as jnp
from jax import lax
from jax.experimental import pallas as pl
from jax.experimental.pallas import tpu as pltpu
from jax.sharding import PartitionSpec as P

SEQ_LEN = 128
VMEM_BYTES = 28 * 2**20
F32 = jnp.float32
BF16 = jnp.bfloat16


def contract(a, b, dim_a, dim_b):
    return lax.dot_general(a, b, (((dim_a,), (dim_b,)), ((), ())), preferred_element_type=F32)


def run_copies(pairs, sem):
    copies = [pltpu.make_async_copy(src, dst, sem.at[j]) for j, (src, dst) in enumerate(pairs)]
    for copy in copies:
        copy.start()
    for copy in copies:
        copy.wait()


def cut_kernel(rows, columns, place, acts, *refs):
    parts, (mine, beside, own, near, skip, across, sem) = refs[:3], refs[3:]
    chip, core = place[0] // 2, place[0] % 2

    def part(m, c):
        first = pl.multiple_of((2 * (chip ^ m) + c) * columns, columns)
        return acts.at[:, pl.ds(first, columns)]

    pairs, at = [], 0
    for x in parts:
        length = x.shape[0]
        pairs.append((x, mine.at[pl.ds(at, length)]))
        pairs.append((x, beside.at[pl.ds(4 * rows + at, length)]))
        at += length
    for m, out in enumerate((own, near, skip, across)):
        pairs.append((part(m, 1 - core), beside.at[pl.ds(m * rows, rows)]))
        pairs.append((part(m, core), out))
    run_copies(pairs, sem)


def cut(me, acts, parts, columns):
    rows = acts.shape[0]
    total = sum(part.shape[0] for part in parts)
    lengths = (total, 4 * rows + total, rows, rows, rows, rows)
    return pl.pallas_call(
        functools.partial(cut_kernel, rows, columns),
        out_shape=[jax.ShapeDtypeStruct((length, columns), BF16) for length in lengths],
        in_specs=[pl.BlockSpec(memory_space=pltpu.SMEM)]
        + [pl.BlockSpec(memory_space=pltpu.HBM)] * (1 + len(parts)),
        out_specs=[pl.BlockSpec(memory_space=pltpu.VMEM)] * len(lengths),
        scratch_shapes=[pltpu.SemaphoreType.DMA((14,))],
    )(me.reshape(1).astype(jnp.int32), acts, *parts)


def join_kernel(rows, beside, *refs):
    parts, outs, sem = refs[:3], refs[3:6], refs[6]
    pairs = [(part, out.at[pl.ds(0, rows)]) for part, out in zip(parts, outs)]
    for m, out in enumerate(outs):
        pairs.append((beside.at[pl.ds((m + 1) * rows, rows)], out.at[pl.ds(rows, rows)]))
    run_copies(pairs, sem)


def join_parts(rows, beside, parts):
    columns = beside.shape[1]
    return pl.pallas_call(
        functools.partial(join_kernel, rows),
        out_shape=[jax.ShapeDtypeStruct((2 * rows, columns), BF16)] * 3,
        in_specs=[pl.BlockSpec(memory_space=pltpu.HBM)] * 4,
        out_specs=[pl.BlockSpec(memory_space=pltpu.VMEM)] * 3,
        scratch_shapes=[pltpu.SemaphoreType.DMA((6,))],
    )(beside, *parts)


def rotate_kernel(count, sizes, sources, parts, place, *refs):
    out, left, basis, grads, sem = refs[parts:]
    copies = []
    for j in range(count):
        for part, (rows, buffer) in enumerate(zip(sizes, (basis, grads, left))):
            array, first = sources[j][part]
            at = pl.multiple_of(place[j] * rows, rows)
            src = refs[array].at[pl.ds(first, rows)]
            copies.append(
                pltpu.make_async_copy(src, buffer.at[pl.ds(at, rows)], sem.at[part, j])
            )
    for copy in copies:
        copy.start()
    for copy in copies:
        copy.wait()
    width = basis.shape[1]
    size = min(width, 256)
    for j in range(0, width, size):
        out[:, j : j + size] = contract(grads[...], basis[:, j : j + size], 1, 0).astype(BF16)


def index_in(arrays, x):
    if not any(x is y for y in arrays):
        arrays.append(x)
    return [x is y for y in arrays].index(True)


def rotate_grads(place, pieces, sizes):
    count = len(pieces)
    width = pieces[0][0][0].shape[1]
    arrays = []
    sources = tuple(tuple((index_in(arrays, x), at) for x, at in piece) for piece in pieces)
    basis_rows, grad_rows, left_rows = (count * rows for rows in sizes)
    return pl.pallas_call(
        functools.partial(rotate_kernel, count, sizes, sources, len(arrays)),
        out_shape=(
            jax.ShapeDtypeStruct((grad_rows, width), BF16),
            jax.ShapeDtypeStruct((left_rows, width), BF16),
        ),
        in_specs=[pl.BlockSpec(memory_space=pltpu.SMEM)]
        + [pl.BlockSpec(memory_space=pltpu.HBM)] * len(arrays),
        out_specs=[pl.BlockSpec(memory_space=pltpu.VMEM)] * 2,
        scratch_shapes=[
            pltpu.VMEM((basis_rows, width), BF16),
            pltpu.VMEM((grad_rows, width), BF16),
            pltpu.SemaphoreType.DMA((3, count)),
        ],
        compiler_params=pltpu.CompilerParams(
            vmem_limit_bytes=8 * 2**20 + 2 * width * (basis_rows + 2 * grad_rows + left_rows)
        ),
        cost_estimate=pl.CostEstimate(
            flops=1,
            bytes_accessed=1,
            transcendentals=0,
        ),
    )(place.astype(jnp.int32), *arrays)


def score_kernel(blocks, parts, queries, info, *refs):
    count = len(blocks)
    arrays = refs[:parts]
    turned, left_in, basis_in, curvature_in, right_in, out = refs[parts : parts + 6]
    acts, rotated, grads, left, basis, curvature, right, sem = refs[parts + 6 :]
    columns, size = basis.shape
    width = curvature.shape[0]
    ranks = right.shape[0]
    step = min(width, 512)

    def acts_copy(q, array, at):
        src = arrays[array].at[pl.ds(at * SEQ_LEN, SEQ_LEN)]
        return pltpu.make_async_copy(src, acts.at[q], sem.at[q])

    def grads_copy(q):
        src = turned.at[pl.ds(pl.multiple_of(info[q] * SEQ_LEN, SEQ_LEN), SEQ_LEN)]
        return pltpu.make_async_copy(src, grads.at[q], sem.at[count + q])

    def curvature_copy(i):
        rows = pl.ds(i * step, step)
        return pltpu.make_async_copy(
            curvature_in.at[rows], curvature.at[rows], sem.at[2 * count + 3 + i]
        )

    basis_copy = pltpu.make_async_copy(basis_in, basis, sem.at[2 * count])
    left_copy = pltpu.make_async_copy(left_in, left, sem.at[2 * count + 1])
    right_copy = pltpu.make_async_copy(right_in, right, sem.at[2 * count + 2])
    basis_copy.start()
    for q, (one, other) in enumerate(blocks):
        if one == other:
            acts_copy(q, *one).start()
        else:
            @pl.when(info[count] == 1)
            def _():
                acts_copy(q, *one).start()

            @pl.when(info[count] == 0)
            def _():
                acts_copy(q, *other).start()
    for q in range(count):
        grads_copy(q).start()
    curvature_copy(0).start()
    right_copy.start()
    left_copy.start()
    for i in range(1, width // step):
        curvature_copy(i).start()
    basis_copy.wait()
    for q, (one, _) in enumerate(blocks):
        acts_copy(q, *one).wait()
        for b in range(columns // size):
            own = slice(b * size, (b + 1) * size)
            rotated[q, :, own] = contract(acts[q, :, own], basis[own, :], 1, 0).astype(BF16)
    for q in range(count):
        grads_copy(q).wait()
    for i in range(width // step):
        rows = slice(i * step, (i + 1) * step)
        curvature_copy(i).wait()
        if i == 0:
            right_copy.wait()
            left_copy.wait()
        inverse = 1.0 / curvature[rows, :].astype(F32)
        weights = left[:, rows].astype(F32)
        for q in range(count):
            scaled = (contract(grads[q, :, rows], rotated[q], 0, 0) * inverse).astype(BF16)
            terms = contract(right[...], scaled, 1, 1) * weights
            total = terms[:, :128]
            for j in range(128, step, 128):
                total = total + terms[:, j : j + 128]
            total = jnp.sum(total.reshape(queries, ranks // queries, 128), axis=1)
            out[q] = total if i == 0 else out[q] + total


def score(sequences, inner, acts, turned, left, basis, curvature, right, queries):
    count = len(acts)
    width, columns = curvature.shape
    ranks = right.shape[0]
    arrays = []

    blocks = tuple(((index_in(arrays, x), i), (index_in(arrays, y), j)) for (x, i), (y, j) in acts)
    info = jnp.concatenate([sequences, inner.reshape(1)]).astype(jnp.int32)
    in_vmem = pl.BlockSpec(memory_space=pltpu.VMEM)
    in_hbm = pl.BlockSpec(memory_space=pltpu.HBM)
    return pl.pallas_call(
        functools.partial(score_kernel, blocks, len(arrays), queries),
        out_shape=jax.ShapeDtypeStruct((count, queries, 128), F32),
        in_specs=[pl.BlockSpec(memory_space=pltpu.SMEM)] + [in_hbm] * (len(arrays) + 5),
        out_specs=in_vmem,
        scratch_shapes=[
            pltpu.VMEM((count, SEQ_LEN, columns), BF16),
            pltpu.VMEM((count, SEQ_LEN, columns), BF16),
            pltpu.VMEM((count, SEQ_LEN, width), BF16),
            pltpu.VMEM(left.shape, BF16),
            pltpu.VMEM(basis.shape, BF16),
            pltpu.VMEM(curvature.shape, BF16),
            pltpu.VMEM(right.shape, BF16),
            pltpu.SemaphoreType.DMA((2 * count + 3 + width // min(width, 512),)),
        ],
        compiler_params=pltpu.CompilerParams(vmem_limit_bytes=VMEM_BYTES),
        cost_estimate=pl.CostEstimate(
            flops=1,
            bytes_accessed=1,
            transcendentals=0,
        ),
    )(info, *arrays, turned, left, basis, curvature, right)


def swap(x, k, n):
    return lax.ppermute(x, "dp", [(i, i ^ k) for i in range(n)])


def hop(x, pairs, cross=False):
    pairs = [(2 * a + c, 2 * b + (c ^ int(cross))) for a, b in pairs for c in range(2)]
    return lax.ppermute(x, "dp", pairs)


def after(x, *others):
    return lax.optimization_barrier((x, *others))[0]


def exchange_line(acts, parts, columns, me, sizes):
    chip, core = me // 2, me % 2
    inner = (chip == 1) | (chip == 2)
    rows = acts.shape[0]
    outward = [(1, 0), (2, 3)]
    mine, to_beside, own, near, skip, across = cut(me, acts, parts, columns)
    second_in = hop(mine, [(1, 2), (2, 1)])
    third_in = hop(mine, [(0, 2), (3, 1)])
    first = hop(mine, [(0, 1), (1, 0), (2, 3), (3, 2)])
    beside = swap(to_beside, 1, 8)
    near, skip, across = join_parts(rows, beside, (near, skip, across))
    near_out = hop(near, outward)
    second_end = hop(after(second_in, first, near_out), outward)
    third_end = hop(third_in, outward)
    across_in = hop(after(across, second_in), [(1, 2), (2, 1)])
    skip_in = hop(after(skip, third_in), [(0, 2), (3, 1)])
    near_in = hop(after(near, first), [(0, 1), (3, 2)])
    skip_out = hop(after(skip, skip_in, across_in), [(1, 3), (2, 0)])
    first_x = swap(first, 1, 8)
    third = jnp.where(inner, third_in, after(third_end, skip_in))
    third_x = swap(third, 1, 8)
    second_end = after(second_end, across_in, near_in)
    second = [
        jnp.where(inner, second_in[: sizes[0]], second_end[: sizes[0]]),
        jnp.where(inner, second_in[sizes[0] :], second_end[sizes[0] :]),
    ]
    second_x = [swap(x, 1, 8) for x in second]
    across_out = hop(after(across, skip_in, across_in, second_end), [(0, 3), (3, 0)])
    chips = jnp.stack(
        [chip, chip ^ 1, jnp.where(inner, chip ^ 3, chip ^ 2), jnp.where(inner, chip ^ 2, chip ^ 3)]
    )
    def whole(x, at=0):
        return [(x, at), (x, at + sizes[0]), (x, at + sizes[0] + sizes[1])]

    def split(x, rest):
        return [(x, 0), (rest, 0), (rest, sizes[1])]

    pieces = [whole(mine), whole(first), split(*second), whole(third)]
    pieces += [whole(beside, 4 * rows), whole(first_x), split(*second_x), whole(third_x)]
    place = jnp.concatenate([2 * chips + core, 2 * chips + 1 - core])
    turned, left = rotate_grads(place, pieces, sizes)
    each = rows // SEQ_LEN
    owners = [me, me ^ 1]
    blocks = [((x, j), (x, j)) for x in (own, beside) for j in range(each)]
    for inside, x, outside, y in (
        (6, (across_in, across_in), 2, (near_out, near_out)),
        (4, (skip_in, skip_in), 4, (skip_out, skip_out)),
        (2, (near_in, near_in), 6, (across_out, across_out)),
    ):
        for c in range(2):
            owners.append(me ^ (jnp.where(inner, inside, outside) + c))
            for j in range(each):
                at = [c * each + j if z[0] is z[1] else j for z in (x, y)]
                blocks.append(((x[c], at[0]), (y[c], at[1])))
    return inner, turned, left, jnp.stack(owners), blocks


def on_device(n, activations, out_grads, in_basis, out_basis, curvature, left_factors, right_factors,
              sequence_ids, query_order):
    me = lax.axis_index("dp")
    acts = activations[0]
    columns = in_basis.shape[1]
    width = out_basis.shape[2]
    left_own = left_factors[0].reshape(-1, width)
    parts = [out_basis[0], out_grads[0], left_own]
    sizes = tuple(part.shape[0] for part in parts)
    right = right_factors[0].reshape(-1, columns)
    queries = right_factors.shape[1]
    each = acts.shape[0] // SEQ_LEN
    if n == 8:
        inner, turned, left, owners, operands = exchange_line(acts, parts, columns, me, sizes)
    else:
        every = lax.all_gather(jnp.concatenate(parts), "dp", axis=0)
        starts = (0, sizes[0], sizes[0] + sizes[1])
        pieces = [[(every[j], at) for at in starts] for j in range(n)]
        place = jnp.arange(n, dtype=jnp.int32)
        turned, left = rotate_grads(place, pieces, sizes)
        part = lax.all_to_all(acts, "dp", split_axis=1, concat_axis=0, tiled=True)
        operands = [((part, j), (part, j)) for j in range(n * each)]
        inner = jnp.bool_(True)
        owners = jnp.arange(n, dtype=jnp.int32)
    sequences = (owners[:, None] * each + jnp.arange(each)[None, :]).reshape(-1).astype(jnp.int32)
    sums = []
    at = 0
    while at < len(operands):
        step = 4 * each
        sums.append(
            score(sequences[at : at + step], inner, operands[at : at + step], turned, left, in_basis[0],
                  curvature[0], right, queries)
        )
        at += step
    scores = jnp.sum(jnp.concatenate(sums), axis=2)
    seqs = scores.shape[0]

    rows = jnp.sum(
        jnp.where(jnp.arange(seqs)[None, :, None] == sequences[:, None, None],
                  sequence_ids[None, :, None], 0), axis=1)
    row_pick = (rows.reshape(1, seqs) == jnp.arange(seqs)[:, None]).astype(F32)
    col_pick = (query_order[:, None] == jnp.arange(queries)[None, :]).astype(F32)
    placed = jnp.dot(jnp.dot(row_pick, scores, precision=lax.Precision.HIGHEST), col_pick,
                     precision=lax.Precision.HIGHEST)
    layers = lax.axis_size("section")
    wanted = jnp.arange(layers) <= lax.axis_index("section")
    outgoing = jnp.where(wanted[:, None, None], placed[None], 0.0)
    outgoing = outgoing.reshape(layers * n, seqs // n, queries)
    arrived = lax.all_to_all(outgoing, ("section", "dp"), split_axis=0, concat_axis=0, tiled=True)
    return jnp.sum(arrived, axis=0)[None]


def solution(mesh):
    placed = (
        P("section", "dp", None),
        P("section", "dp", None),
        P("section", "dp", None),
        P("section", "dp", None),
        P("section", None, "dp"),
        P("section", "dp", None, None),
        P("section", None, None, "dp"),
        P(),
        P(),
    )
    return jax.shard_map(
        functools.partial(on_device, mesh.shape["dp"]), mesh=mesh, in_specs=placed,
        out_specs=P("section", "dp", None), check_vma=False,
    )
```

```python
import functools

import jax
import jax.numpy as jnp
from jax import lax
from jax.experimental import pallas as pl
from jax.experimental.pallas import tpu as pltpu
from jax.sharding import PartitionSpec as P

SEQ_LEN = 128
VMEM_BYTES = 28 * 2**20
F32 = jnp.float32
BF16 = jnp.bfloat16


def contract(a, b, dim_a, dim_b):
    return lax.dot_general(a, b, (((dim_a,), (dim_b,)), ((), ())), preferred_element_type=F32)


def run_copies(pairs, sem):
    copies = [pltpu.make_async_copy(src, dst, sem.at[j]) for j, (src, dst) in enumerate(pairs)]
    for copy in copies:
        copy.start()
    for copy in copies:
        copy.wait()


def cut_kernel(rows, columns, place, acts, *refs):
    parts, (mine, beside, sem) = refs[:3], refs[3:]
    chip, core = place[0] // 2, place[0] % 2

    def part(m, c):
        first = pl.multiple_of((2 * (chip ^ m) + c) * columns, columns)
        return acts.at[:, pl.ds(first, columns)]

    pairs, at = [], 0
    for x in parts:
        length = x.shape[0]
        pairs.append((x, mine.at[pl.ds(at, length)]))
        pairs.append((x, beside.at[pl.ds(4 * rows + at, length)]))
        at += length
    for m in range(4):
        pairs.append((part(m, 1 - core), beside.at[pl.ds(m * rows, rows)]))
    run_copies(pairs, sem)


def cut(me, acts, parts, columns):
    rows = acts.shape[0]
    total = sum(part.shape[0] for part in parts)
    lengths = (total, 4 * rows + total)
    return pl.pallas_call(
        functools.partial(cut_kernel, rows, columns),
        out_shape=[jax.ShapeDtypeStruct((length, columns), BF16) for length in lengths],
        in_specs=[pl.BlockSpec(memory_space=pltpu.SMEM)]
        + [pl.BlockSpec(memory_space=pltpu.HBM)] * (1 + len(parts)),
        out_specs=[pl.BlockSpec(memory_space=pltpu.VMEM)] * len(lengths),
        scratch_shapes=[pltpu.SemaphoreType.DMA((10,))],
    )(me.reshape(1).astype(jnp.int32), acts, *parts)


def join_kernel(rows, columns, place, acts, beside, own, *refs):
    outs, sem = refs[:3], refs[3]
    chip, core = place[0] // 2, place[0] % 2
    pairs = []
    for m, out in enumerate((own, *outs)):
        first = pl.multiple_of((2 * (chip ^ m) + core) * columns, columns)
        pairs.append((acts.at[:, pl.ds(first, columns)], out.at[pl.ds(0, rows)]))
        if m:
            pairs.append((beside.at[pl.ds(m * rows, rows)], out.at[pl.ds(rows, rows)]))
    run_copies(pairs, sem)


def join_parts(me, acts, beside, columns):
    rows = acts.shape[0]
    lengths = (rows, 2 * rows, 2 * rows, 2 * rows)
    return pl.pallas_call(
        functools.partial(join_kernel, rows, columns),
        out_shape=[jax.ShapeDtypeStruct((length, columns), BF16) for length in lengths],
        in_specs=[pl.BlockSpec(memory_space=pltpu.SMEM)]
        + [pl.BlockSpec(memory_space=pltpu.HBM)] * 2,
        out_specs=[pl.BlockSpec(memory_space=pltpu.VMEM)] * 4,
        scratch_shapes=[pltpu.SemaphoreType.DMA((7,))],
    )(me.reshape(1).astype(jnp.int32), acts, beside)


def rotate_kernel(count, sizes, sources, parts, place, *refs):
    out, left, basis, grads, sem = refs[parts:]
    copies = []
    for j in range(count):
        for part, (rows, buffer) in enumerate(zip(sizes, (basis, grads, left))):
            array, first = sources[j][part]
            at = pl.multiple_of(place[j] * rows, rows)
            src = refs[array].at[pl.ds(first, rows)]
            copies.append(
                pltpu.make_async_copy(src, buffer.at[pl.ds(at, rows)], sem.at[part, j])
            )
    for copy in copies:
        copy.start()
    for copy in copies:
        copy.wait()
    width = basis.shape[1]
    size = min(width, 256)
    for j in range(0, width, size):
        out[:, j : j + size] = contract(grads[...], basis[:, j : j + size], 1, 0).astype(BF16)


def index_in(arrays, x):
    if not any(x is y for y in arrays):
        arrays.append(x)
    return [x is y for y in arrays].index(True)


def rotate_grads(place, pieces, sizes):
    count = len(pieces)
    width = pieces[0][0][0].shape[1]
    arrays = []
    sources = tuple(tuple((index_in(arrays, x), at) for x, at in piece) for piece in pieces)
    basis_rows, grad_rows, left_rows = (count * rows for rows in sizes)
    return pl.pallas_call(
        functools.partial(rotate_kernel, count, sizes, sources, len(arrays)),
        out_shape=(
            jax.ShapeDtypeStruct((grad_rows, width), BF16),
            jax.ShapeDtypeStruct((left_rows, width), BF16),
        ),
        in_specs=[pl.BlockSpec(memory_space=pltpu.SMEM)]
        + [pl.BlockSpec(memory_space=pltpu.HBM)] * len(arrays),
        out_specs=[pl.BlockSpec(memory_space=pltpu.VMEM)] * 2,
        scratch_shapes=[
            pltpu.VMEM((basis_rows, width), BF16),
            pltpu.VMEM((grad_rows, width), BF16),
            pltpu.SemaphoreType.DMA((3, count)),
        ],
        compiler_params=pltpu.CompilerParams(
            vmem_limit_bytes=8 * 2**20 + 2 * width * (basis_rows + 2 * grad_rows + left_rows)
        ),
        cost_estimate=pl.CostEstimate(
            flops=1,
            bytes_accessed=1,
            transcendentals=0,
        ),
    )(place.astype(jnp.int32), *arrays)


def score_kernel(blocks, parts, queries, info, *refs):
    count = len(blocks)
    arrays = refs[:parts]
    turned, left_in, basis_in, curvature_in, right_in, out = refs[parts : parts + 6]
    acts, rotated, grads, left, basis, curvature, right, sem = refs[parts + 6 :]
    columns, size = basis.shape
    width = curvature.shape[0]
    ranks = right.shape[0]
    step = min(width, 512)

    def acts_copy(q, array, at):
        src = arrays[array].at[pl.ds(at * SEQ_LEN, SEQ_LEN)]
        return pltpu.make_async_copy(src, acts.at[q], sem.at[q])

    def grads_copy(q):
        src = turned.at[pl.ds(pl.multiple_of(info[q] * SEQ_LEN, SEQ_LEN), SEQ_LEN)]
        return pltpu.make_async_copy(src, grads.at[q], sem.at[count + q])

    def curvature_copy(i):
        rows = pl.ds(i * step, step)
        return pltpu.make_async_copy(
            curvature_in.at[rows], curvature.at[rows], sem.at[2 * count + 3 + i]
        )

    basis_copy = pltpu.make_async_copy(basis_in, basis, sem.at[2 * count])
    left_copy = pltpu.make_async_copy(left_in, left, sem.at[2 * count + 1])
    right_copy = pltpu.make_async_copy(right_in, right, sem.at[2 * count + 2])
    basis_copy.start()
    for q, (one, other) in enumerate(blocks):
        if one == other:
            acts_copy(q, *one).start()
        else:
            @pl.when(info[count] == 1)
            def _():
                acts_copy(q, *one).start()

            @pl.when(info[count] == 0)
            def _():
                acts_copy(q, *other).start()
    for q in range(count):
        grads_copy(q).start()
    curvature_copy(0).start()
    right_copy.start()
    left_copy.start()
    for i in range(1, width // step):
        curvature_copy(i).start()
    basis_copy.wait()
    for q, (one, _) in enumerate(blocks):
        acts_copy(q, *one).wait()
        for b in range(columns // size):
            own = slice(b * size, (b + 1) * size)
            rotated[q, :, own] = contract(acts[q, :, own], basis[own, :], 1, 0).astype(BF16)
    for q in range(count):
        grads_copy(q).wait()
    for i in range(width // step):
        rows = slice(i * step, (i + 1) * step)
        curvature_copy(i).wait()
        if i == 0:
            right_copy.wait()
            left_copy.wait()
        inverse = 1.0 / curvature[rows, :].astype(F32)
        weights = left[:, rows].astype(F32)
        for q in range(count):
            scaled = (contract(grads[q, :, rows], rotated[q], 0, 0) * inverse).astype(BF16)
            terms = contract(right[...], scaled, 1, 1) * weights
            total = terms[:, :128]
            for j in range(128, step, 128):
                total = total + terms[:, j : j + 128]
            total = jnp.sum(total.reshape(queries, ranks // queries, 128), axis=1)
            out[q] = total if i == 0 else out[q] + total


def score(sequences, inner, acts, turned, left, basis, curvature, right, queries):
    count = len(acts)
    width, columns = curvature.shape
    ranks = right.shape[0]
    arrays = []

    blocks = tuple(((index_in(arrays, x), i), (index_in(arrays, y), j)) for (x, i), (y, j) in acts)
    info = jnp.concatenate([sequences, inner.reshape(1)]).astype(jnp.int32)
    in_vmem = pl.BlockSpec(memory_space=pltpu.VMEM)
    in_hbm = pl.BlockSpec(memory_space=pltpu.HBM)
    return pl.pallas_call(
        functools.partial(score_kernel, blocks, len(arrays), queries),
        out_shape=jax.ShapeDtypeStruct((count, queries, 128), F32),
        in_specs=[pl.BlockSpec(memory_space=pltpu.SMEM)] + [in_hbm] * (len(arrays) + 5),
        out_specs=in_vmem,
        scratch_shapes=[
            pltpu.VMEM((count, SEQ_LEN, columns), BF16),
            pltpu.VMEM((count, SEQ_LEN, columns), BF16),
            pltpu.VMEM((count, SEQ_LEN, width), BF16),
            pltpu.VMEM(left.shape, BF16),
            pltpu.VMEM(basis.shape, BF16),
            pltpu.VMEM(curvature.shape, BF16),
            pltpu.VMEM(right.shape, BF16),
            pltpu.SemaphoreType.DMA((2 * count + 3 + width // min(width, 512),)),
        ],
        compiler_params=pltpu.CompilerParams(vmem_limit_bytes=VMEM_BYTES),
        cost_estimate=pl.CostEstimate(
            flops=1,
            bytes_accessed=1,
            transcendentals=0,
        ),
    )(info, *arrays, turned, left, basis, curvature, right)


def swap(x, k, n):
    return lax.ppermute(x, "dp", [(i, i ^ k) for i in range(n)])


def hop(x, pairs, cross=False):
    pairs = [(2 * a + c, 2 * b + (c ^ int(cross))) for a, b in pairs for c in range(2)]
    return lax.ppermute(x, "dp", pairs)


def after(x, *others):
    return lax.optimization_barrier((x, *others))[0]


def exchange_line(acts, parts, columns, me, sizes):
    chip, core = me // 2, me % 2
    inner = (chip == 1) | (chip == 2)
    rows = acts.shape[0]
    outward = [(1, 0), (2, 3)]
    mine, to_beside = cut(me, acts, parts, columns)
    second_in = hop(mine, [(1, 2), (2, 1)])
    third_in = hop(mine, [(0, 2), (3, 1)])
    first = hop(mine, [(0, 1), (1, 0), (2, 3), (3, 2)])
    beside = swap(to_beside, 1, 8)
    own, near, skip, across = join_parts(me, acts, beside, columns)
    near_out = hop(near, outward)
    second_end = hop(after(second_in, first, near_out), outward)
    third_end = hop(third_in, outward)
    across_in = hop(after(across, second_in), [(1, 2), (2, 1)])
    skip_in = hop(after(skip, third_in), [(0, 2), (3, 1)])
    near_in = hop(after(near, first), [(0, 1), (3, 2)])
    skip_out = hop(after(skip, skip_in, across_in), [(1, 3), (2, 0)])
    first_x = swap(first, 1, 8)
    third = jnp.where(inner, third_in, after(third_end, skip_in))
    third_x = swap(third, 1, 8)
    second_end = after(second_end, across_in, near_in)
    second = [
        jnp.where(inner, second_in[: sizes[0]], second_end[: sizes[0]]),
        jnp.where(inner, second_in[sizes[0] :], second_end[sizes[0] :]),
    ]
    second_x = [swap(x, 1, 8) for x in second]
    across_out = hop(after(across, skip_in, across_in, second_end), [(0, 3), (3, 0)])
    chips = jnp.stack(
        [chip, chip ^ 1, jnp.where(inner, chip ^ 3, chip ^ 2), jnp.where(inner, chip ^ 2, chip ^ 3)]
    )
    def whole(x, at=0):
        return [(x, at), (x, at + sizes[0]), (x, at + sizes[0] + sizes[1])]

    def split(x, rest):
        return [(x, 0), (rest, 0), (rest, sizes[1])]

    pieces = [whole(mine), whole(first), split(*second), whole(third)]
    pieces += [whole(beside, 4 * rows), whole(first_x), split(*second_x), whole(third_x)]
    place = jnp.concatenate([2 * chips + core, 2 * chips + 1 - core])
    turned, left = rotate_grads(place, pieces, sizes)
    each = rows // SEQ_LEN
    owners = [me, me ^ 1]
    blocks = [((x, j), (x, j)) for x in (own, beside) for j in range(each)]
    for inside, x, outside, y in (
        (6, (across_in, across_in), 2, (near_out, near_out)),
        (4, (skip_in, skip_in), 4, (skip_out, skip_out)),
        (2, (near_in, near_in), 6, (across_out, across_out)),
    ):
        for c in range(2):
            owners.append(me ^ (jnp.where(inner, inside, outside) + c))
            for j in range(each):
                at = [c * each + j if z[0] is z[1] else j for z in (x, y)]
                blocks.append(((x[c], at[0]), (y[c], at[1])))
    return inner, turned, left, jnp.stack(owners), blocks


def on_device(n, activations, out_grads, in_basis, out_basis, curvature, left_factors, right_factors,
              sequence_ids, query_order):
    me = lax.axis_index("dp")
    acts = activations[0]
    columns = in_basis.shape[1]
    width = out_basis.shape[2]
    left_own = left_factors[0].reshape(-1, width)
    parts = [out_basis[0], out_grads[0], left_own]
    sizes = tuple(part.shape[0] for part in parts)
    right = right_factors[0].reshape(-1, columns)
    queries = right_factors.shape[1]
    each = acts.shape[0] // SEQ_LEN
    if n == 8:
        inner, turned, left, owners, operands = exchange_line(acts, parts, columns, me, sizes)
    else:
        every = lax.all_gather(jnp.concatenate(parts), "dp", axis=0)
        starts = (0, sizes[0], sizes[0] + sizes[1])
        pieces = [[(every[j], at) for at in starts] for j in range(n)]
        place = jnp.arange(n, dtype=jnp.int32)
        turned, left = rotate_grads(place, pieces, sizes)
        part = lax.all_to_all(acts, "dp", split_axis=1, concat_axis=0, tiled=True)
        operands = [((part, j), (part, j)) for j in range(n * each)]
        inner = jnp.bool_(True)
        owners = jnp.arange(n, dtype=jnp.int32)
    sequences = (owners[:, None] * each + jnp.arange(each)[None, :]).reshape(-1).astype(jnp.int32)
    sums = []
    at = 0
    while at < len(operands):
        step = 4 * each
        sums.append(
            score(sequences[at : at + step], inner, operands[at : at + step], turned, left, in_basis[0],
                  curvature[0], right, queries)
        )
        at += step
    scores = jnp.sum(jnp.concatenate(sums), axis=2)
    seqs = scores.shape[0]

    rows = jnp.sum(
        jnp.where(jnp.arange(seqs)[None, :, None] == sequences[:, None, None],
                  sequence_ids[None, :, None], 0), axis=1)
    row_pick = (rows.reshape(1, seqs) == jnp.arange(seqs)[:, None]).astype(F32)
    col_pick = (query_order[:, None] == jnp.arange(queries)[None, :]).astype(F32)
    placed = jnp.dot(jnp.dot(row_pick, scores, precision=lax.Precision.HIGHEST), col_pick,
                     precision=lax.Precision.HIGHEST)
    layers = lax.axis_size("section")
    wanted = jnp.arange(layers) <= lax.axis_index("section")
    outgoing = jnp.where(wanted[:, None, None], placed[None], 0.0)
    outgoing = outgoing.reshape(layers * n, seqs // n, queries)
    arrived = lax.all_to_all(outgoing, ("section", "dp"), split_axis=0, concat_axis=0, tiled=True)
    return jnp.sum(arrived, axis=0)[None]


def solution(mesh):
    placed = (
        P("section", "dp", None),
        P("section", "dp", None),
        P("section", "dp", None),
        P("section", "dp", None),
        P("section", None, "dp"),
        P("section", "dp", None, None),
        P("section", None, None, "dp"),
        P(),
        P(),
    )
    return jax.shard_map(
        functools.partial(on_device, mesh.shape["dp"]), mesh=mesh, in_specs=placed,
        out_specs=P("section", "dp", None), check_vma=False,
    )
```

```python
import functools

import jax
import jax.numpy as jnp
from jax import lax
from jax.experimental import pallas as pl
from jax.experimental.pallas import tpu as pltpu
from jax.sharding import PartitionSpec as P

SEQ_LEN = 128
VMEM_BYTES = 28 * 2**20
F32 = jnp.float32
BF16 = jnp.bfloat16


def contract(a, b, dim_a, dim_b):
    return lax.dot_general(a, b, (((dim_a,), (dim_b,)), ((), ())), preferred_element_type=F32)


def run_copies(pairs, sem):
    copies = [pltpu.make_async_copy(src, dst, sem.at[j]) for j, (src, dst) in enumerate(pairs)]
    for copy in copies:
        copy.start()
    for copy in copies:
        copy.wait()


def cut_kernel(rows, columns, place, acts, *refs):
    parts, (mine, beside, sem) = refs[:3], refs[3:]
    chip, core = place[0] // 2, place[0] % 2

    def part(m, c):
        first = pl.multiple_of((2 * (chip ^ m) + c) * columns, columns)
        return acts.at[:, pl.ds(first, columns)]

    pairs, at = [], 0
    for x in parts:
        length = x.shape[0]
        pairs.append((x, mine.at[pl.ds(at, length)]))
        pairs.append((x, beside.at[pl.ds(4 * rows + at, length)]))
        at += length
    for m in range(4):
        pairs.append((part(m, 1 - core), beside.at[pl.ds(m * rows, rows)]))
    run_copies(pairs, sem)


def cut(me, acts, parts, columns):
    rows = acts.shape[0]
    total = sum(part.shape[0] for part in parts)
    lengths = (total, 4 * rows + total)
    return pl.pallas_call(
        functools.partial(cut_kernel, rows, columns),
        out_shape=[jax.ShapeDtypeStruct((length, columns), BF16) for length in lengths],
        in_specs=[pl.BlockSpec(memory_space=pltpu.SMEM)]
        + [pl.BlockSpec(memory_space=pltpu.HBM)] * (1 + len(parts)),
        out_specs=[pl.BlockSpec(memory_space=pltpu.VMEM)] * len(lengths),
        scratch_shapes=[pltpu.SemaphoreType.DMA((10,))],
    )(me.reshape(1).astype(jnp.int32), acts, *parts)


def join_kernel(rows, columns, place, acts, beside, own, *refs):
    outs, sem = refs[:3], refs[3]
    chip, core = place[0] // 2, place[0] % 2
    pairs = []
    for m, out in enumerate((own, *outs)):
        first = pl.multiple_of((2 * (chip ^ m) + core) * columns, columns)
        pairs.append((acts.at[:, pl.ds(first, columns)], out.at[pl.ds(0, rows)]))
        if m:
            pairs.append((beside.at[pl.ds(m * rows, rows)], out.at[pl.ds(rows, rows)]))
    run_copies(pairs, sem)


def join_parts(me, acts, beside, columns):
    rows = acts.shape[0]
    lengths = (rows, 2 * rows, 2 * rows, 2 * rows)
    return pl.pallas_call(
        functools.partial(join_kernel, rows, columns),
        out_shape=[jax.ShapeDtypeStruct((length, columns), BF16) for length in lengths],
        in_specs=[pl.BlockSpec(memory_space=pltpu.SMEM)]
        + [pl.BlockSpec(memory_space=pltpu.HBM)] * 2,
        out_specs=[pl.BlockSpec(memory_space=pltpu.VMEM)] * 4,
        scratch_shapes=[pltpu.SemaphoreType.DMA((7,))],
    )(me.reshape(1).astype(jnp.int32), acts, beside)


def rotate_kernel(count, sizes, sources, parts, place, *refs):
    out, left, basis, grads, sem = refs[parts:]
    copies = []
    for j in range(count):
        for part, (rows, buffer) in enumerate(zip(sizes, (basis, grads, left))):
            array, first = sources[j][part]
            at = pl.multiple_of(place[j] * rows, rows)
            src = refs[array].at[pl.ds(first, rows)]
            copies.append(
                pltpu.make_async_copy(src, buffer.at[pl.ds(at, rows)], sem.at[part, j])
            )
    for copy in copies:
        copy.start()
    for copy in copies:
        copy.wait()
    width = basis.shape[1]
    size = min(width, 256)
    for j in range(0, width, size):
        out[:, j : j + size] = contract(grads[...], basis[:, j : j + size], 1, 0).astype(BF16)


def index_in(arrays, x):
    if not any(x is y for y in arrays):
        arrays.append(x)
    return [x is y for y in arrays].index(True)


def rotate_grads(place, pieces, sizes):
    count = len(pieces)
    width = pieces[0][0][0].shape[1]
    arrays = []
    sources = tuple(tuple((index_in(arrays, x), at) for x, at in piece) for piece in pieces)
    basis_rows, grad_rows, left_rows = (count * rows for rows in sizes)
    return pl.pallas_call(
        functools.partial(rotate_kernel, count, sizes, sources, len(arrays)),
        out_shape=(
            jax.ShapeDtypeStruct((grad_rows, width), BF16),
            jax.ShapeDtypeStruct((left_rows, width), BF16),
        ),
        in_specs=[pl.BlockSpec(memory_space=pltpu.SMEM)]
        + [pl.BlockSpec(memory_space=pltpu.HBM)] * len(arrays),
        out_specs=[pl.BlockSpec(memory_space=pltpu.VMEM)] * 2,
        scratch_shapes=[
            pltpu.VMEM((basis_rows, width), BF16),
            pltpu.VMEM((grad_rows, width), BF16),
            pltpu.SemaphoreType.DMA((3, count)),
        ],
        compiler_params=pltpu.CompilerParams(
            vmem_limit_bytes=8 * 2**20 + 2 * width * (basis_rows + 2 * grad_rows + left_rows)
        ),
        cost_estimate=pl.CostEstimate(
            flops=1,
            bytes_accessed=1,
            transcendentals=0,
        ),
    )(place.astype(jnp.int32), *arrays)


def score_kernel(blocks, parts, queries, info, *refs):
    count = len(blocks)
    arrays = refs[:parts]
    turned, left_in, basis_in, curvature_in, right_in, out = refs[parts : parts + 6]
    acts, rotated, grads, left, basis, curvature, right, sem = refs[parts + 6 :]
    columns, size = basis.shape
    width = curvature.shape[0]
    ranks = right.shape[0]
    step = min(width, 1024)

    def acts_copy(q, array, at):
        src = arrays[array].at[pl.ds(at * SEQ_LEN, SEQ_LEN)]
        return pltpu.make_async_copy(src, acts.at[q], sem.at[q])

    def grads_copy(q):
        src = turned.at[pl.ds(pl.multiple_of(info[q] * SEQ_LEN, SEQ_LEN), SEQ_LEN)]
        return pltpu.make_async_copy(src, grads.at[q], sem.at[count + q])

    def curvature_copy(i):
        rows = pl.ds(i * step, step)
        return pltpu.make_async_copy(
            curvature_in.at[rows], curvature.at[rows], sem.at[2 * count + 3 + i]
        )

    basis_copy = pltpu.make_async_copy(basis_in, basis, sem.at[2 * count])
    left_copy = pltpu.make_async_copy(left_in, left, sem.at[2 * count + 1])
    right_copy = pltpu.make_async_copy(right_in, right, sem.at[2 * count + 2])
    basis_copy.start()
    for q, (one, other) in enumerate(blocks):
        if one == other:
            acts_copy(q, *one).start()
        else:
            @pl.when(info[count] == 1)
            def _():
                acts_copy(q, *one).start()

            @pl.when(info[count] == 0)
            def _():
                acts_copy(q, *other).start()
    for q in range(count):
        grads_copy(q).start()
    curvature_copy(0).start()
    right_copy.start()
    left_copy.start()
    for i in range(1, width // step):
        curvature_copy(i).start()
    basis_copy.wait()
    for q, (one, _) in enumerate(blocks):
        acts_copy(q, *one).wait()
        for b in range(columns // size):
            own = slice(b * size, (b + 1) * size)
            rotated[q, :, own] = contract(acts[q, :, own], basis[own, :], 1, 0).astype(BF16)
    for q in range(count):
        grads_copy(q).wait()
    for i in range(width // step):
        rows = slice(i * step, (i + 1) * step)
        curvature_copy(i).wait()
        if i == 0:
            right_copy.wait()
            left_copy.wait()
        inverse = 1.0 / curvature[rows, :].astype(F32)
        weights = left[:, rows].astype(F32)
        for q in range(count):
            scaled = (contract(grads[q, :, rows], rotated[q], 0, 0) * inverse).astype(BF16)
            terms = contract(right[...], scaled, 1, 1) * weights
            total = terms[:, :128]
            for j in range(128, step, 128):
                total = total + terms[:, j : j + 128]
            total = jnp.sum(total.reshape(queries, ranks // queries, 128), axis=1)
            out[q] = total if i == 0 else out[q] + total


def score(sequences, inner, acts, turned, left, basis, curvature, right, queries):
    count = len(acts)
    width, columns = curvature.shape
    ranks = right.shape[0]
    arrays = []

    blocks = tuple(((index_in(arrays, x), i), (index_in(arrays, y), j)) for (x, i), (y, j) in acts)
    info = jnp.concatenate([sequences, inner.reshape(1)]).astype(jnp.int32)
    in_vmem = pl.BlockSpec(memory_space=pltpu.VMEM)
    in_hbm = pl.BlockSpec(memory_space=pltpu.HBM)
    return pl.pallas_call(
        functools.partial(score_kernel, blocks, len(arrays), queries),
        out_shape=jax.ShapeDtypeStruct((count, queries, 128), F32),
        in_specs=[pl.BlockSpec(memory_space=pltpu.SMEM)] + [in_hbm] * (len(arrays) + 5),
        out_specs=in_vmem,
        scratch_shapes=[
            pltpu.VMEM((count, SEQ_LEN, columns), BF16),
            pltpu.VMEM((count, SEQ_LEN, columns), BF16),
            pltpu.VMEM((count, SEQ_LEN, width), BF16),
            pltpu.VMEM(left.shape, BF16),
            pltpu.VMEM(basis.shape, BF16),
            pltpu.VMEM(curvature.shape, BF16),
            pltpu.VMEM(right.shape, BF16),
            pltpu.SemaphoreType.DMA((2 * count + 3 + width // min(width, 1024),)),
        ],
        compiler_params=pltpu.CompilerParams(vmem_limit_bytes=VMEM_BYTES),
        cost_estimate=pl.CostEstimate(
            flops=1,
            bytes_accessed=1,
            transcendentals=0,
        ),
    )(info, *arrays, turned, left, basis, curvature, right)


def swap(x, k, n):
    return lax.ppermute(x, "dp", [(i, i ^ k) for i in range(n)])


def hop(x, pairs, cross=False):
    pairs = [(2 * a + c, 2 * b + (c ^ int(cross))) for a, b in pairs for c in range(2)]
    return lax.ppermute(x, "dp", pairs)


def after(x, *others):
    return lax.optimization_barrier((x, *others))[0]


def exchange_line(acts, parts, columns, me, sizes):
    chip, core = me // 2, me % 2
    inner = (chip == 1) | (chip == 2)
    rows = acts.shape[0]
    outward = [(1, 0), (2, 3)]
    mine, to_beside = cut(me, acts, parts, columns)
    second_in = hop(mine, [(1, 2), (2, 1)])
    third_in = hop(mine, [(0, 2), (3, 1)])
    first = hop(mine, [(0, 1), (1, 0), (2, 3), (3, 2)])
    beside = swap(to_beside, 1, 8)
    own, near, skip, across = join_parts(me, acts, beside, columns)
    near_out = hop(near, outward)
    second_end = hop(after(second_in, first, near_out), outward)
    third_end = hop(third_in, outward)
    across_in = hop(after(across, second_in), [(1, 2), (2, 1)])
    skip_in = hop(after(skip, third_in), [(0, 2), (3, 1)])
    near_in = hop(after(near, first), [(0, 1), (3, 2)])
    skip_out = hop(after(skip, skip_in, across_in), [(1, 3), (2, 0)])
    first_x = swap(first, 1, 8)
    third = jnp.where(inner, third_in, after(third_end, skip_in))
    third_x = swap(third, 1, 8)
    second_end = after(second_end, across_in, near_in)
    second = [
        jnp.where(inner, second_in[: sizes[0]], second_end[: sizes[0]]),
        jnp.where(inner, second_in[sizes[0] :], second_end[sizes[0] :]),
    ]
    second_x = [swap(x, 1, 8) for x in second]
    across_out = hop(after(across, skip_in, across_in, second_end), [(0, 3), (3, 0)])
    chips = jnp.stack(
        [chip, chip ^ 1, jnp.where(inner, chip ^ 3, chip ^ 2), jnp.where(inner, chip ^ 2, chip ^ 3)]
    )
    def whole(x, at=0):
        return [(x, at), (x, at + sizes[0]), (x, at + sizes[0] + sizes[1])]

    def split(x, rest):
        return [(x, 0), (rest, 0), (rest, sizes[1])]

    pieces = [whole(mine), whole(first), split(*second), whole(third)]
    pieces += [whole(beside, 4 * rows), whole(first_x), split(*second_x), whole(third_x)]
    place = jnp.concatenate([2 * chips + core, 2 * chips + 1 - core])
    turned, left = rotate_grads(place, pieces, sizes)
    each = rows // SEQ_LEN
    owners = [me, me ^ 1]
    blocks = [((x, j), (x, j)) for x in (own, beside) for j in range(each)]
    for inside, x, outside, y in (
        (6, (across_in, across_in), 2, (near_out, near_out)),
        (4, (skip_in, skip_in), 4, (skip_out, skip_out)),
        (2, (near_in, near_in), 6, (across_out, across_out)),
    ):
        for c in range(2):
            owners.append(me ^ (jnp.where(inner, inside, outside) + c))
            for j in range(each):
                at = [c * each + j if z[0] is z[1] else j for z in (x, y)]
                blocks.append(((x[c], at[0]), (y[c], at[1])))
    return inner, turned, left, jnp.stack(owners), blocks


def on_device(n, activations, out_grads, in_basis, out_basis, curvature, left_factors, right_factors,
              sequence_ids, query_order):
    me = lax.axis_index("dp")
    acts = activations[0]
    columns = in_basis.shape[1]
    width = out_basis.shape[2]
    left_own = left_factors[0].reshape(-1, width)
    parts = [out_basis[0], out_grads[0], left_own]
    sizes = tuple(part.shape[0] for part in parts)
    right = right_factors[0].reshape(-1, columns)
    queries = right_factors.shape[1]
    each = acts.shape[0] // SEQ_LEN
    if n == 8:
        inner, turned, left, owners, operands = exchange_line(acts, parts, columns, me, sizes)
    else:
        every = lax.all_gather(jnp.concatenate(parts), "dp", axis=0)
        starts = (0, sizes[0], sizes[0] + sizes[1])
        pieces = [[(every[j], at) for at in starts] for j in range(n)]
        place = jnp.arange(n, dtype=jnp.int32)
        turned, left = rotate_grads(place, pieces, sizes)
        part = lax.all_to_all(acts, "dp", split_axis=1, concat_axis=0, tiled=True)
        operands = [((part, j), (part, j)) for j in range(n * each)]
        inner = jnp.bool_(True)
        owners = jnp.arange(n, dtype=jnp.int32)
    sequences = (owners[:, None] * each + jnp.arange(each)[None, :]).reshape(-1).astype(jnp.int32)
    sums = []
    at = 0
    while at < len(operands):
        step = 4 * each
        sums.append(
            score(sequences[at : at + step], inner, operands[at : at + step], turned, left, in_basis[0],
                  curvature[0], right, queries)
        )
        at += step
    scores = jnp.sum(jnp.concatenate(sums), axis=2)
    seqs = scores.shape[0]

    rows = jnp.sum(
        jnp.where(jnp.arange(seqs)[None, :, None] == sequences[:, None, None],
                  sequence_ids[None, :, None], 0), axis=1)
    row_pick = (rows.reshape(1, seqs) == jnp.arange(seqs)[:, None]).astype(F32)
    col_pick = (query_order[:, None] == jnp.arange(queries)[None, :]).astype(F32)
    placed = jnp.dot(jnp.dot(row_pick, scores, precision=lax.Precision.HIGHEST), col_pick,
                     precision=lax.Precision.HIGHEST)
    layers = lax.axis_size("section")
    wanted = jnp.arange(layers) <= lax.axis_index("section")
    outgoing = jnp.where(wanted[:, None, None], placed[None], 0.0)
    outgoing = outgoing.reshape(layers * n, seqs // n, queries)
    arrived = lax.all_to_all(outgoing, ("section", "dp"), split_axis=0, concat_axis=0, tiled=True)
    return jnp.sum(arrived, axis=0)[None]


def solution(mesh):
    placed = (
        P("section", "dp", None),
        P("section", "dp", None),
        P("section", "dp", None),
        P("section", "dp", None),
        P("section", None, "dp"),
        P("section", "dp", None, None),
        P("section", None, None, "dp"),
        P(),
        P(),
    )
    return jax.shard_map(
        functools.partial(on_device, mesh.shape["dp"]), mesh=mesh, in_specs=placed,
        out_specs=P("section", "dp", None), check_vma=False,
    )
```
